128 devices in a mesh: section: 8 (over y_lo, z), seq: 16 (over y_hi, x, core).
Axes of the slice: x: 4, y: 4 (y_hi: 2, y_lo: 2; y = y_hi * 2 + y_lo), z: 4, core: 2. Of those that a mesh axis runs over, the one named last changes fastest.
Arguments:
- x_a: bfloat16 [2048, 4096], P('seq'), may hold values from -6 to 6
- x_b: bfloat16 [2048, 4096], P('seq'), may hold values from -6 to 6
- grad_a: bfloat16 [2048, 4096], P('seq'), may hold values from -6 to 6
- grad_b: bfloat16 [2048, 4096], P('seq'), may hold values from -6 to 6
- gains: float32 [8, 2, 4096], P('section'), may hold values from 0.5 to 1.5
- kv_weights: bfloat16 [8, 2, 4096, 1024], P('section'), may hold values from -0.09375 to 0.09375
- doc_lengths: int32 [2, 32], replicated, may hold values from 1 to 128, 2048 in all within a row
Outputs:
- acts: bfloat16 [2, 8, 2048, 4096], P(None, 'section', 'seq')
- in_grads: bfloat16 [2, 8, 2048, 4096], P(None, 'section', 'seq')
- kv_grads: bfloat16 [2, 8, 2048, 1024], P(None, 'section', 'seq')
The draws below stay inside these ranges and needn't reach their ends.
Inputs may be any that keep to these rules, and one draw needn't show every extreme that they name: `doc_lengths`: each row lists 32 documents that fill the 2048 tokens of its sequence in order; in each row some document is exactly 128 tokens long.
All inputs are finite; a program needn't handle non-finite values.
Results may differ from the reference program's by a relative error of at most 0.024.
Values may be sent and summed in bfloat16 or wider, within the bound.
No kernel may reach another device: no remote copies, remote signals or barrier semaphores. Data moves between devices by JAX's collectives and lax.ppermute only.
A program may use at most 320 MiB of HBM per device.

```python
import math
import jax
import jax.numpy as jnp
import numpy as np
from jax import lax

HEADS = 32
HEAD_DIM = 128
KV_HEADS = 4
REACH = 1
TOK_DEV = 128
D = 4096
KV_WIDTH = 1024
TOKENS = 2048
DOCS = 32
N_SECTION = 8
N_SEQ = 16


def block_scale(own_key, shape, pieces, smallest, high):
    def one(axis_at, blocks):
        steps = jax.random.uniform(jax.random.fold_in(jax.random.fold_in(own_key, 6), axis_at), (blocks,), jnp.float32, smallest / len(pieces), high / len(pieces))
        return jnp.repeat(jnp.exp(steps), shape[axis_at] // blocks).reshape((-1,) + (1,) * (len(shape) - axis_at - 1))

    level = one(*pieces[0])
    for cut in pieces[1:]:
        level = level * one(*cut)
    return level


def profile(count, total, reach, lean):
    portions = [(1 << 20) // math.isqrt(grade ** lean) + 1 for grade in range(2, count + 1)]
    rest, given = total - reach - (count - 1), [1] * (count - 1)
    while rest > 0:
        candidates = [i for i in range(count - 1) if given[i] < reach]
        whole, left = sum([portions[i] for i in candidates]), rest
        for i in candidates:
            addition = min(reach - given[i], max(1, left * portions[i] // whole), rest)
            given[i] = given[i] + addition
            rest = rest - addition
    return np.array([reach] + given)


def uneven(stream_key, count, total, bound, slope):
    if count == 2:
        one = jax.random.randint(stream_key, (), max(1, total - bound), min(bound, total - 1) + 1)
        return jnp.stack([one, total - one])
    tallies = jnp.asarray(profile(count, total, bound, slope), jnp.int32)
    twos = (count - 1) // 2
    donor, taker = tallies[1:1 + 2 * twos:2], tallies[2:2 + 2 * twos:2]
    slack = jnp.minimum(donor - 1, bound - taker)
    moved = jax.random.randint(jax.random.fold_in(stream_key, 1), (twos,), 0, 1 << 20) % (slack + 1)
    tallies = tallies.at[1:1 + 2 * twos:2].set(donor - moved).at[2:2 + 2 * twos:2].set(taker + moved)
    return tallies[jax.random.permutation(jax.random.fold_in(stream_key, 2), count)]


def bell_draw(own_key, extent, spread, most, cuts=(), held_as=jnp.bfloat16):
    result = jax.random.normal(own_key, extent, jnp.float32) * spread
    if len(cuts) > 0:
        result = block_scale(own_key, extent, cuts, -0.22, 0.18) * result
    return jnp.clip(result, min=-most, max=most).astype(held_as)


def setup_inputs(seed: int = 0) -> dict:
    key_of = jax.random.split(jax.random.key(seed), 8)
    x_a = bell_draw(key_of[0], (TOKENS, D), 1.0, 6.0, ((0, 16),))
    x_b = bell_draw(key_of[1], (TOKENS, D), 1.0, 6.0, ((0, 16),))
    grad_a = bell_draw(key_of[2], (TOKENS, D), 1.0, 6.0, ((0, 16),))
    grad_b = bell_draw(key_of[3], (TOKENS, D), 1.0, 6.0, ((0, 16),))
    gains = jnp.clip(1.0 + 0.1 * jax.random.normal(key_of[4], (N_SECTION, 2, D), jnp.float32), 0.5, 1.5)
    kv_weights = bell_draw(key_of[5], (N_SECTION, 2, D, KV_WIDTH), D ** -0.5, 0.09375, ((0, 8),))
    doc_lengths = jax.vmap(lambda own: uneven(own, DOCS, TOKENS, REACH * TOK_DEV, 1))(jax.random.split(key_of[6], 2)).reshape((2, DOCS)).astype(jnp.int32)
    return {"x_a": x_a, "x_b": x_b, "grad_a": grad_a, "grad_b": grad_b, "gains": gains, "kv_weights": kv_weights, "doc_lengths": doc_lengths}


epsilon = 1e-05

def normalize(stream, gain_row):
    widened = stream.astype(jnp.float32)
    square_mean = lax.optimization_barrier(jnp.mean(widened * widened, axis=-1, keepdims=True))
    return (widened * lax.rsqrt(square_mean + epsilon) * gain_row).astype(jnp.bfloat16)

def project_kv(stream, gain_row, weight_mat):
    return jnp.dot(normalize(stream, gain_row), weight_mat, preferred_element_type=jnp.float32).astype(jnp.bfloat16)

def doc_index(ends_row, places):
    return lax.optimization_barrier(jnp.sum((ends_row[None, :] <= places[:, None]).astype(jnp.int32), axis=1)).astype(jnp.int32)

def mix(stream, gain_row, pair_rows, docs_query, place_query, docs_key, place_key):
    row_count = stream.shape[0]
    widened = stream.astype(jnp.float32)
    normed = normalize(stream, gain_row)
    group_size = HEADS // KV_HEADS
    queries = normed.reshape(row_count, KV_HEADS, group_size, HEAD_DIM).astype(jnp.float32)
    key_count = pair_rows.shape[0]
    key_heads = pair_rows[:, :KV_HEADS * HEAD_DIM].reshape(key_count, KV_HEADS, HEAD_DIM).astype(jnp.float32)
    value_heads = pair_rows[:, KV_HEADS * HEAD_DIM:].reshape(key_count, KV_HEADS, HEAD_DIM).astype(jnp.float32)
    scores = jnp.einsum('tkgd,skd->kgts', queries, key_heads) * (1.0 / math.sqrt(HEAD_DIM))
    allowed = (docs_query[:, None] == docs_key[None, :]) & (place_key[None, :] <= place_query[:, None]) & (place_key[None, :] >= 0)
    scores = jnp.where(allowed, scores, -1e+30)
    largest = lax.optimization_barrier(jnp.max(scores, axis=-1, keepdims=True))
    powers = jnp.exp(scores - largest)
    weights = (powers / lax.optimization_barrier(jnp.sum(powers, axis=-1, keepdims=True))).astype(jnp.bfloat16)
    mixture = jnp.einsum('kgts,skd->tkgd', weights.astype(jnp.float32), value_heads)
    return (widened + mixture.reshape(row_count, HEADS * HEAD_DIM)).astype(jnp.bfloat16)

def whole_mix(stream, key_values, gain_row, ends_row):
    width = key_values.shape[-1]
    padded = jnp.concatenate([jnp.zeros((REACH * TOK_DEV, width), key_values.dtype), key_values], axis=0)

    def one_block(block):
        start = (block * TOK_DEV).astype(jnp.int32)
        rows = lax.dynamic_slice_in_dim(stream, start, TOK_DEV, 0)
        pairs = lax.dynamic_slice_in_dim(padded, start, (REACH + 1) * TOK_DEV, 0)
        query_places = (start + jnp.arange(TOK_DEV, dtype=jnp.int32)).astype(jnp.int32)
        key_places = (start - REACH * TOK_DEV + jnp.arange((REACH + 1) * TOK_DEV, dtype=jnp.int32)).astype(jnp.int32)
        return mix(rows, gain_row, pairs, doc_index(ends_row, query_places), query_places, doc_index(ends_row, key_places), key_places)
    outputs = lax.map(one_block, jnp.arange(N_SEQ, dtype=jnp.int32))
    return outputs.reshape(TOKENS, stream.shape[-1])

def reference(x_a, x_b, grad_a, grad_b, gains, kv_weights, doc_lengths):
    acts_all = []
    inputs_all = []
    pairs_all = []
    for direction in range(2):
        ends_row = jnp.cumsum(doc_lengths[direction]).astype(jnp.int32)
        stream = (x_a, x_b)[direction]
        cotangent = (grad_a, grad_b)[direction]
        owners = [layer_index if direction == 0 else N_SECTION - 1 - layer_index for layer_index in range(N_SECTION)]
        inputs_kept = []
        acts_by = [None] * N_SECTION
        ingrad_by = [None] * N_SECTION
        kvgrad_by = [None] * N_SECTION
        for layer_index in range(N_SECTION):
            owner_section = owners[layer_index]
            gain_row = gains[owner_section, direction]
            weight_mat = kv_weights[owner_section, direction]
            inputs_kept.append(stream)
            key_values = project_kv(stream, gain_row, weight_mat)
            stream = whole_mix(stream, key_values, gain_row, ends_row)
            acts_by[owner_section] = stream
        for layer_index in reversed(range(N_SECTION)):
            owner_section = owners[layer_index]
            gain_row = gains[owner_section, direction]
            weight_mat = kv_weights[owner_section, direction]
            layer_input = inputs_kept[layer_index]
            key_values = project_kv(layer_input, gain_row, weight_mat)
            _, pull_mix = jax.vjp(lambda stream_arg, pairs_arg: whole_mix(stream_arg, pairs_arg, gain_row, ends_row), layer_input, key_values)
            grad_stream, grad_pairs = pull_mix(cotangent)
            _, pull_proj = jax.vjp(lambda stream_arg: project_kv(stream_arg, gain_row, weight_mat), layer_input)
            cotangent = grad_stream + pull_proj(grad_pairs)[0]
            ingrad_by[owner_section] = cotangent
            kvgrad_by[owner_section] = grad_pairs
        acts_all.append(jnp.stack(acts_by))
        inputs_all.append(jnp.stack(ingrad_by))
        pairs_all.append(jnp.stack(kvgrad_by))
    return (jnp.stack(acts_all), jnp.stack(inputs_all), jnp.stack(pairs_all))
```

```python
import functools
import math

import jax
import jax.numpy as jnp
from jax import lax
from jax.experimental import pallas as pl
from jax.experimental.pallas import tpu as pltpu
from jax.sharding import PartitionSpec as P

HEADS = 32
HEAD_DIM = 128
KV_HEADS = 4
LAYERS = 8
GROUP = HEADS // KV_HEADS
ROWS = 128
COLS = GROUP * HEAD_DIM
WIDTH = 2 * KV_HEADS * HEAD_DIM
D = HEADS * HEAD_DIM
QUARTER = COLS // 4
STAT = 16
STATE = COLS + 3 * HEAD_DIM
SCALE = 1.0 / math.sqrt(HEAD_DIM)
epsilon = 1e-05

BF = jnp.bfloat16
F32 = jnp.float32
AXES = ("section", "seq")
VMEM_LIMIT = 48 * 1024 * 1024


def route(target):
    pairs = []
    for section in range(8):
        for shard in range(16):
            there = target(section, shard)
            pairs.append((section * 16 + shard, there[0] * 16 + there[1]))
    return pairs


def to_section(k, flip=False):
    return route(lambda s, q: (s ^ k, q ^ (8 if flip and q & 1 else 0)))


def to_shard(step):
    return route(lambda s, q: (s, (q + step) % 16))


def to_mate():
    return route(lambda s, q: (s, q ^ 1))


def to_beside():
    return route(lambda s, q: (s, q ^ (6 if q & 1 else 2)))


def send(block, pairs):
    return lax.ppermute(block, AXES, pairs)


def eye_mask(n):
    return lax.broadcasted_iota(jnp.int32, (n, n), 0) == lax.broadcasted_iota(jnp.int32, (n, n), 1)


def as_row(column):
    n = column.shape[0]
    return jnp.sum(jnp.where(eye_mask(n), column, 0.0), axis=0, keepdims=True)


def as_column(row):
    n = row.shape[1]
    return jnp.sum(jnp.where(eye_mask(n), row, 0.0), axis=1, keepdims=True)


def split_rows(row):
    high = row.astype(BF).astype(F32)
    low = row - high
    at = lax.broadcasted_iota(jnp.int32, (STAT, row.shape[1]), 0)
    return jnp.where(at == 0, high, jnp.where(at == 1, low, 0.0)).astype(BF)


def stack_heads(block):
    return jnp.concatenate([block[:, i * HEAD_DIM : (i + 1) * HEAD_DIM] for i in range(GROUP)], axis=0)


def unstack_heads(block, rows):
    return jnp.concatenate([block[i * rows : (i + 1) * rows] for i in range(GROUP)], axis=1)


def dot_nt(a, b):
    return lax.dot_general(a, b, (((1,), (1,)), ((), ())), preferred_element_type=F32)


def dot_tn(a, b):
    return lax.dot_general(a, b, (((0,), (0,)), ((), ())), preferred_element_type=F32)


def softmax_of(queries, keys, bias):
    scores = dot_nt(queries, keys) * SCALE
    scores = scores.reshape(GROUP, ROWS, -1) + bias[None]
    powers = jnp.exp(scores - jnp.max(scores, axis=-1, keepdims=True))
    weights = powers * (1.0 / jnp.sum(powers, axis=-1, keepdims=True))
    return weights.reshape(GROUP * ROWS, -1)


def load_weights(layer, info, w_refs, w_buf, g_buf, sems, act):
    low = layer < LAYERS // 2
    k_here, role, direction = info[layer], info[8], info[9]
    for k in range(4):
        blocks = w_refs[4 * (k - 1) + 2 : 4 * (k - 1) + 6] if low else w_refs[4 * k : 4 * k + 4]

        @pl.when(k_here == (k if low else k + 4))
        def _():
            if low and k == 0:
                rows = pl.ds(pl.multiple_of(role * COLS, COLS), COLS)
                act(pltpu.make_async_copy(w_refs[0].at[0, direction, rows], w_buf, sems.at[0]))
                if g_buf is not None:
                    act(pltpu.make_async_copy(w_refs[1], g_buf, sems.at[4]))
            else:
                for j, block in enumerate(blocks):
                    there = pl.ds(pl.multiple_of(info[10 + j] * QUARTER, QUARTER), QUARTER)
                    act(pltpu.make_async_copy(block.at[:QUARTER], w_buf.at[there], sems.at[j]))
                if g_buf is not None:
                    act(pltpu.make_async_copy(blocks[0].at[QUARTER:], g_buf, sems.at[4]))


def start_copy(copy):
    copy.start()


def wait_copy(copy):
    copy.wait()


def project(h, gain, info, w_buf, flat, out):
    wide = h.astype(F32)
    flat[...] = jnp.dot((wide * gain).astype(BF), w_buf[...], preferred_element_type=F32)
    stats = split_rows(as_row(jnp.sum(wide * wide, axis=1, keepdims=True)))
    role = info[8]
    for k in range(4):
        head = jnp.bitwise_xor(role, k)
        at_key = pl.ds(pl.multiple_of(head * HEAD_DIM, HEAD_DIM), HEAD_DIM)
        at_value = pl.ds(pl.multiple_of((head + KV_HEADS) * HEAD_DIM, HEAD_DIM), HEAD_DIM)
        out[k, : 2 * ROWS, :HEAD_DIM] = flat[:, at_key].astype(BF)
        out[k, : 2 * ROWS, HEAD_DIM:] = flat[:, at_value].astype(BF)
        out[k, 2 * ROWS :, :] = stats


def add_parts(parts):
    total = parts[0].astype(F32)
    for part in parts[1:]:
        total = total + part.astype(F32)
    return total


def forward_kernel(layer, n_w, *refs):
    attend, projects = layer >= 0, layer + 1 < LAYERS
    at = 0
    info = refs[0]
    h_ref = refs[1]
    at = 2
    if attend:
        gain_ref, parts, bias_ref = refs[at], refs[at + 1 : at + 5], refs[at + 5]
        at += 6
    if projects:
        w_refs = refs[at : at + n_w]
        at += n_w
    if attend:
        h_out, state_out, kvprev_out = refs[at : at + 3]
        at += 3
    if projects:
        piece_out = refs[at]
        gain_out = refs[at + 1]
        w_buf, g_buf, flat, sems = refs[at + 2 : at + 6]
        load_weights(layer + 1, info, w_refs, w_buf, g_buf, sems, start_copy)
    h = h_ref[...]
    if attend:
        total = add_parts([p[...] for p in parts])
        ss = total[2 * ROWS : 2 * ROWS + 1] + total[2 * ROWS + 1 : 2 * ROWS + 2]
        inv = as_column(lax.rsqrt(ss * (1.0 / D) + epsilon))
        kv = (total[: 2 * ROWS] * inv).astype(BF)
        wide = h.astype(F32)
        queries = (wide * inv * gain_ref[:1]).astype(BF)
        inv_high = inv.astype(BF).astype(F32)
        inv_low = inv - inv_high
        lane = lax.broadcasted_iota(jnp.int32, (ROWS, HEAD_DIM), 1)
        state_out[:, :COLS] = h[ROWS:]
        state_out[:, COLS : COLS + 2 * HEAD_DIM] = kv[ROWS:]
        state_out[:, COLS + 2 * HEAD_DIM :] = jnp.where(
            lane < HEAD_DIM // 2, inv_high[ROWS:], inv_low[ROWS:]
        ).astype(BF)
        kvprev_out[...] = kv[:ROWS]
        keys, values = kv[:, :HEAD_DIM], kv[:, HEAD_DIM:]
        before = softmax_of(stack_heads(queries[:ROWS]), keys[:ROWS], bias_ref[0][:, ROWS:]).astype(BF)
        mixed = jnp.dot(before, values[:ROWS], preferred_element_type=F32)
        h_out[:ROWS] = (wide[:ROWS] + unstack_heads(mixed, ROWS)).astype(BF)
        own = softmax_of(stack_heads(queries[ROWS:]), keys, bias_ref[1]).astype(BF)
        mixed = jnp.dot(own, values, preferred_element_type=F32)
        h_out[ROWS:] = (wide[ROWS:] + unstack_heads(mixed, ROWS)).astype(BF)
        h = h_out[...] if projects else None
    if projects:
        load_weights(layer + 1, info, w_refs, w_buf, g_buf, sems, wait_copy)
        terms = g_buf[...].astype(F32)
        gain = terms[0:1] + terms[1:2] + terms[2:3]
        gain_out[...] = jnp.broadcast_to(gain, gain_out.shape)
        project(h, gain, info, w_buf, flat, piece_out)


def state_parts(own, following):
    h = jnp.concatenate([own[:, :COLS], following[:, :COLS]], axis=0).astype(F32)
    stat = jnp.concatenate([own[:, COLS + 2 * HEAD_DIM :], following[:, COLS + 2 * HEAD_DIM :]], axis=0)
    stat = stat.astype(F32)
    inv = stat[:, :1] + stat[:, HEAD_DIM // 2 : HEAD_DIM // 2 + 1]
    return h, inv


def attend_back(queries, cotangent, keys, values, bias):
    weights = softmax_of(queries, keys, bias)
    grad_weights = dot_nt(cotangent, values).astype(BF).astype(F32)
    inner = jnp.sum(weights * grad_weights, axis=1, keepdims=True)
    grad_scores = (weights * (grad_weights - inner) * SCALE).astype(BF)
    return weights.astype(BF), grad_scores


def backward_kernel(layer, n_w, *refs):
    finish, attend = layer + 1 < LAYERS, layer >= 0
    info, d_ref = refs[:2]
    at = 2
    if finish:
        gain_up, dq_ref = refs[at : at + 2]
        at += 1
        parts = refs[at + 1 : at + 5]
        up_own, up_next = refs[at + 5 : at + 7]
        w_refs = refs[at + 7 : at + 7 + n_w]
        at += 7 + n_w
    if attend:
        gain_ref, own_ref, next_ref, prev_ref, bias_ref = refs[at : at + 5]
        at += 5
    if finish:
        out_ref = refs[at]
        at += 1
    if attend:
        if finish:
            d_out = refs[at]
            at += 1
        dq_out, piece_out = refs[at : at + 2]
        at += 2
    if finish:
        w_buf, flat, sems = refs[at : at + 3]
        load_weights(layer + 1, info, w_refs, w_buf, None, sems, start_copy)
        role = info[8]
        stats = jnp.zeros((1, 2 * ROWS), F32)
        for k in range(4):
            head = jnp.bitwise_xor(role, k)
            at_key = pl.ds(pl.multiple_of(head * HEAD_DIM, HEAD_DIM), HEAD_DIM)
            at_value = pl.ds(pl.multiple_of((head + KV_HEADS) * HEAD_DIM, HEAD_DIM), HEAD_DIM)
            flat[:, at_key] = parts[k][: 2 * ROWS, :HEAD_DIM]
            flat[:, at_value] = parts[k][: 2 * ROWS, HEAD_DIM:]
            tail = parts[k][2 * ROWS :, :].astype(F32)
            stats = stats + tail[0:1] + tail[1:2]
        shift = as_column(stats * (1.0 / D))
        h, inv = state_parts(up_own, up_next)
        base = d_ref[...].astype(F32) - h * (inv * inv * shift)
        base_gain = gain_up[:1]
        load_weights(layer + 1, info, w_refs, w_buf, None, sems, wait_copy)
        grad = dot_nt(flat[...], w_buf[...]) + dq_ref[...].astype(F32)
        d = (base + grad * base_gain * inv).astype(BF)
        out_ref[:, :COLS] = d[:ROWS]
        out_ref[:, COLS:] = parts[0][:ROWS, :]
        if attend:
            d_out[...] = d
    else:
        d = d_ref[...]
    if attend:
        h, inv = state_parts(own_ref, next_ref)
        queries = (h * inv * gain_ref[:1]).astype(BF)
        kv_own = own_ref[:, COLS : COLS + 2 * HEAD_DIM]
        kv_next = next_ref[:, COLS : COLS + 2 * HEAD_DIM]
        kv_prev = prev_ref[...]
        stat = []
        q0, d0 = stack_heads(queries[:ROWS]), stack_heads(d[:ROWS])
        kv0 = jnp.concatenate([kv_prev, kv_own], axis=0)
        w0, s0 = attend_back(q0, d0, kv0[:, :HEAD_DIM], kv0[:, HEAD_DIM:], bias_ref[1])
        dq0 = unstack_heads(jnp.dot(s0, kv0[:, :HEAD_DIM], preferred_element_type=F32), ROWS).astype(BF)
        dk_own = dot_tn(s0[:, ROWS:], q0)
        dv_own = dot_tn(w0[:, ROWS:], d0)
        q1, d1 = stack_heads(queries[ROWS:]), stack_heads(d[ROWS:])
        kv1 = jnp.concatenate([kv_own, kv_next], axis=0)
        w1, s1 = attend_back(q1, d1, kv1[:, :HEAD_DIM], kv1[:, HEAD_DIM:], bias_ref[2])
        dq1 = unstack_heads(jnp.dot(s1, kv1[:, :HEAD_DIM], preferred_element_type=F32), ROWS).astype(BF)
        dk = dot_tn(s1, q1)
        dv = dot_tn(w1, d1)
        dkv_own = jnp.concatenate([dk_own + dk[:ROWS], dv_own + dv[:ROWS]], axis=1).astype(BF)
        dkv_next = jnp.concatenate([dk[ROWS:], dv[ROWS:]], axis=1).astype(BF)
        dq_out[:ROWS] = dq0
        dq_out[ROWS:] = dq1
        dkv = jnp.concatenate([dkv_own, dkv_next], axis=0)
        dq = jnp.concatenate([dq0, dq1], axis=0)
        column = jnp.sum(dq.astype(F32) * queries.astype(F32), axis=1, keepdims=True)
        column = column + jnp.sum(dkv.astype(F32) * kv1.astype(F32), axis=1, keepdims=True)
        piece_out[: 2 * ROWS, :] = dkv
        piece_out[2 * ROWS :, :] = split_rows(as_row(column))


SMEM_SPEC = pl.BlockSpec(memory_space=pltpu.SMEM)
VMEM_SPEC = pl.BlockSpec(memory_space=pltpu.VMEM)
GAIN = (8, COLS)
ANY_SPEC = pl.BlockSpec(memory_space=pl.ANY)


def call(kernel, operands, specs, outs, scratch, flops):
    return pl.pallas_call(
        kernel,
        out_shape=[jax.ShapeDtypeStruct(shape, F32 if shape == GAIN else BF) for shape in outs],
        in_specs=specs,
        out_specs=[VMEM_SPEC] * len(outs),
        scratch_shapes=scratch,
        compiler_params=pltpu.CompilerParams(vmem_limit_bytes=VMEM_LIMIT),
        cost_estimate=pl.CostEstimate(flops=flops, bytes_accessed=4 << 20, transcendentals=0),
    )(*operands)


def forward_call(layer, info, h, gain, parts, bias, weights):
    attend, projects = layer >= 0, layer + 1 < LAYERS
    operands, specs = [info, h], [SMEM_SPEC, VMEM_SPEC]
    outs, scratch, n_w = [], [], 0
    if attend:
        operands += [gain] + list(parts) + [bias]
        specs += [VMEM_SPEC] * 6
        outs += [(2 * ROWS, COLS), (ROWS, STATE), (ROWS, 2 * HEAD_DIM)]
    if projects:
        w_refs = weights[(layer + 1) // 4]
        n_w = len(w_refs)
        operands += w_refs
        specs += [ANY_SPEC] * n_w
        outs += [(4, 2 * ROWS + STAT, 2 * HEAD_DIM), GAIN]
        scratch = [
            pltpu.VMEM((COLS, WIDTH), BF),
            pltpu.VMEM((STAT, COLS), BF),
            pltpu.VMEM((2 * ROWS, WIDTH), F32),
            pltpu.SemaphoreType.DMA((5,)),
        ]
    return call(functools.partial(forward_kernel, layer, n_w), operands, specs, outs, scratch, 2 << 30)


def backward_call(layer, info, d, gains, dq, parts, up, here, kvprev, bias, weights):
    finish, attend = layer + 1 < LAYERS, layer >= 0
    operands, specs = [info, d], [SMEM_SPEC, VMEM_SPEC]
    outs, scratch, n_w = [], [], 0
    if finish:
        w_refs = weights[(layer + 1) // 4]
        n_w = len(w_refs)
        operands += [gains[layer + 1], dq] + list(parts) + list(up) + w_refs
        specs += [VMEM_SPEC] * 8 + [ANY_SPEC] * n_w
        outs += [(ROWS, COLS + 2 * HEAD_DIM)]
        scratch = [
            pltpu.VMEM((COLS, WIDTH), BF),
            pltpu.VMEM((2 * ROWS, WIDTH), BF),
            pltpu.SemaphoreType.DMA((5,)),
        ]
    if attend:
        operands += [gains[layer]] + list(here) + [kvprev, bias]
        specs += [VMEM_SPEC] * 5
        if finish:
            outs += [(2 * ROWS, COLS)]
        outs += [(2 * ROWS, COLS), (2 * ROWS + STAT, 2 * HEAD_DIM)]
    return call(functools.partial(backward_kernel, layer, n_w), operands, specs, outs, scratch, 4 << 30)


def pick(blocks, index):
    return lax.select_n(index, *blocks)


def deliver(messages, section, low):
    upper = section // 4
    here = lax.rem(section, 4)
    got = []
    for k in range(4):
        target = jnp.bitwise_xor(section, k + low)
        layer = jnp.where(upper == 0, target, LAYERS - 1 - target) - low
        block = pick(messages, layer)
        got.append(block if k + low == 0 else send(block, to_section(k + low)))
    return [pick(got, jnp.bitwise_xor(here, role)) for role in range(4)]


def per_device(x_a, x_b, grad_a, grad_b, gains, kv_weights, doc_lengths):
    section = lax.axis_index("section").astype(jnp.int32)
    shard = lax.axis_index("seq").astype(jnp.int32)
    upper = section // 4
    role = lax.rem(section, 4)
    core = lax.rem(shard, 2)
    first = upper == 0

    parity = lax.rem(shard // 2, 2)

    layers = jnp.arange(LAYERS, dtype=jnp.int32)
    holders = jnp.where(first, layers, LAYERS - 1 - layers)
    quarter = 2 * parity + core
    arrival = jnp.stack([quarter, jnp.bitwise_xor(quarter, 2), jnp.bitwise_xor(quarter, 1), 3 - quarter])
    info = jnp.concatenate([jnp.bitwise_xor(section, holders), jnp.stack([role, upper]), arrival, jnp.zeros((2,), jnp.int32)])

    high = lax.reduce_precision(gains[0], 8, 7)
    middle = lax.reduce_precision(gains[0] - high, 8, 7)
    terms = jnp.stack([high, middle, gains[0] - high - middle]).astype(BF)
    terms = jnp.pad(terms, ((0, STAT - 3), (0, 0), (0, 0)))

    def gain_block(target):
        return lax.dynamic_slice(terms, (0, target // 4, lax.rem(target, 4) * COLS), (STAT, 1, COLS))[:, 0]

    def message(k):
        target = jnp.bitwise_xor(section, k)
        start = lax.rem(target, 4) * COLS + quarter * QUARTER
        rows = lax.dynamic_slice(kv_weights, (0, target // 4, start, 0), (1, 1, QUARTER, WIDTH))[0, 0]
        return jnp.concatenate([rows, gain_block(target)], axis=0)

    def spread(mine):
        beside = send(mine, to_beside())
        return [mine, beside, send(mine, to_mate()), send(beside, to_mate())]

    near = [send(message(k), to_section(k)) for k in range(1, 4)]
    far_messages = [message(k) for k in range(4, 8)]
    far = [send(block, to_section(k, flip=True)) for k, block in zip(range(4, 8), far_messages)]
    weights = (
        [kv_weights, gain_block(section)] + [w for block in near for w in spread(block)],
        [w for block in far for w in spread(block)],
    )

    lengths = jnp.where(first, doc_lengths[0], doc_lengths[1])
    which = jnp.arange(lengths.shape[0])
    ends = jnp.sum(jnp.where(which[None, :] <= which[:, None], lengths[None, :], 0), axis=1)
    places = (shard - 2) * ROWS + jnp.arange(4 * ROWS, dtype=jnp.int32)
    docs = jnp.sum((ends[None, :] <= places[:, None]).astype(jnp.int32), axis=1)
    docs = jnp.where(places < 0, -1, docs)
    bias = []
    for block in range(3):
        q_place, q_doc = places[(block + 1) * ROWS : (block + 2) * ROWS], docs[(block + 1) * ROWS : (block + 2) * ROWS]
        k_place, k_doc = places[block * ROWS : (block + 2) * ROWS], docs[block * ROWS : (block + 2) * ROWS]
        allowed = (q_doc[:, None] == k_doc[None, :]) & (k_place[None, :] <= q_place[:, None])
        bias.append(jnp.where(allowed, 0.0, -1e30).astype(F32))
    bias = jnp.stack(bias)

    columns = role * COLS
    x_own = lax.dynamic_slice(jnp.where(first, x_a, x_b), (0, columns), (ROWS, COLS))
    grad_own = lax.dynamic_slice(jnp.where(first, grad_a, grad_b), (0, columns), (ROWS, COLS))
    h = jnp.concatenate([send(x_own, to_shard(1)), x_own], axis=0)
    cotangent = jnp.concatenate([grad_own, send(grad_own, to_shard(-1))], axis=0)

    def exchange(pieces):
        return [pieces[0]] + [send(pieces[k], to_section(k)) for k in range(1, 4)]

    pieces, gain = forward_call(-1, info, h, None, None, bias, weights)
    states, befores, acts, gain_rows = [], [], [], [gain]
    for layer in range(LAYERS):
        parts = exchange([pieces[k] for k in range(4)])
        out = forward_call(layer, info, h, gain_rows[layer], parts, bias, weights)
        h, state, before = out[:3]
        if layer + 1 < LAYERS:
            pieces = out[3]
            gain_rows.append(out[4])
        states.append((state, send(state, to_shard(-1))))
        befores.append(before)
        acts.append(h[ROWS:])

    act_sets = [deliver(acts[:4], section, 0), deliver(acts[4:], section, 4)]

    d = cotangent
    dq, piece = backward_call(
        LAYERS - 1, info, d, gain_rows, None, None, None, states[-1], befores[-1], bias, weights
    )
    grads = [None] * LAYERS
    for layer in range(LAYERS - 2, -2, -1):
        parts = exchange([piece] * 4)
        here = states[layer] if layer >= 0 else None
        before = befores[layer] if layer >= 0 else None
        out = backward_call(
            layer, info, d, gain_rows, dq, parts, states[layer + 1], here, before, bias, weights
        )
        grads[layer + 1] = out[0]
        if layer >= 0:
            d, dq, piece = out[1:]
    grad_sets = [deliver(grads[:4], section, 0), deliver(grads[4:], section, 4)]

    def assemble(sets, cut):
        near = jnp.concatenate([cut(b) for b in sets[0]], axis=1)
        far = jnp.concatenate([cut(b) for b in sets[1]], axis=1)
        return jnp.stack([jnp.where(first, near, far), jnp.where(first, far, near)])[:, None]

    acts_out = assemble(act_sets, lambda b: b)
    ingrad_out = assemble(grad_sets, lambda b: b[:, :COLS])
    keys = assemble(grad_sets, lambda b: b[:, COLS : COLS + HEAD_DIM])
    values = assemble(grad_sets, lambda b: b[:, COLS + HEAD_DIM :])
    return acts_out, ingrad_out, jnp.concatenate([keys, values], axis=-1)


def solution(mesh):
    in_specs = (
        P("seq", None),
        P("seq", None),
        P("seq", None),
        P("seq", None),
        P("section", None, None),
        P("section", None, None, None),
        P(),
    )
    out_specs = (
        P(None, "section", "seq", None),
        P(None, "section", "seq", None),
        P(None, "section", "seq", None),
    )
    return jax.shard_map(
        per_device, mesh=mesh, in_specs=in_specs, out_specs=out_specs, check_vma=False
    )
```

```python
import functools
import math

import jax
import jax.numpy as jnp
from jax import lax
from jax.experimental import pallas as pl
from jax.experimental.pallas import tpu as pltpu
from jax.sharding import PartitionSpec as P

HEADS = 32
HEAD_DIM = 128
KV_HEADS = 4
LAYERS = 8
GROUP = HEADS // KV_HEADS
ROWS = 128
COLS = GROUP * HEAD_DIM
WIDTH = 2 * KV_HEADS * HEAD_DIM
D = HEADS * HEAD_DIM
QUARTER = COLS // 4
STAT = 16
STATE = COLS + 3 * HEAD_DIM
SCALE = 1.0 / math.sqrt(HEAD_DIM)
epsilon = 1e-05

BF = jnp.bfloat16
F32 = jnp.float32
AXES = ("section", "seq")
VMEM_LIMIT = 48 * 1024 * 1024


def route(target):
    pairs = []
    for section in range(8):
        for shard in range(16):
            there = target(section, shard)
            pairs.append((section * 16 + shard, there[0] * 16 + there[1]))
    return pairs


def to_section(k, flip=False):
    return route(lambda s, q: (s ^ k, q ^ (8 if flip and q & 1 else 0)))


def to_shard(step):
    return route(lambda s, q: (s, (q + step) % 16))


def to_mate():
    return route(lambda s, q: (s, q ^ 1))


def to_beside():
    return route(lambda s, q: (s, q ^ (6 if q & 1 else 2)))


def send(block, pairs):
    return lax.ppermute(block, AXES, pairs)


def eye_mask(n):
    return lax.broadcasted_iota(jnp.int32, (n, n), 0) == lax.broadcasted_iota(jnp.int32, (n, n), 1)


def as_row(column):
    n = column.shape[0]
    return jnp.sum(jnp.where(eye_mask(n), column, 0.0), axis=0, keepdims=True)


def as_column(row):
    n = row.shape[1]
    return jnp.sum(jnp.where(eye_mask(n), row, 0.0), axis=1, keepdims=True)


def split_rows(row):
    high = row.astype(BF).astype(F32)
    low = row - high
    at = lax.broadcasted_iota(jnp.int32, (STAT, row.shape[1]), 0)
    return jnp.where(at == 0, high, jnp.where(at == 1, low, 0.0)).astype(BF)


def stack_heads(block):
    return jnp.concatenate([block[:, i * HEAD_DIM : (i + 1) * HEAD_DIM] for i in range(GROUP)], axis=0)


def unstack_heads(block, rows):
    return jnp.concatenate([block[i * rows : (i + 1) * rows] for i in range(GROUP)], axis=1)


def dot_nt(a, b):
    return lax.dot_general(a, b, (((1,), (1,)), ((), ())), preferred_element_type=F32)


def dot_tn(a, b):
    return lax.dot_general(a, b, (((0,), (0,)), ((), ())), preferred_element_type=F32)


def softmax_of(queries, keys, bias):
    scores = dot_nt(queries, keys) * SCALE
    scores = scores.reshape(GROUP, ROWS, -1) + bias[None]
    powers = jnp.exp(scores - jnp.max(scores, axis=-1, keepdims=True))
    weights = powers * (1.0 / jnp.sum(powers, axis=-1, keepdims=True))
    return weights.reshape(GROUP * ROWS, -1)


def load_weights(layer, info, w_refs, w_buf, g_buf, sems, act):
    low = layer < LAYERS // 2
    k_here, role, direction = info[layer], info[8], info[9]
    for k in range(4):
        blocks = w_refs[4 * (k - 1) + 2 : 4 * (k - 1) + 6] if low else w_refs[4 * k : 4 * k + 4]

        @pl.when(k_here == (k if low else k + 4))
        def _():
            if low and k == 0:
                rows = pl.ds(pl.multiple_of(role * COLS, COLS), COLS)
                act(pltpu.make_async_copy(w_refs[0].at[0, direction, rows], w_buf, sems.at[0]))
                if g_buf is not None:
                    act(pltpu.make_async_copy(w_refs[1], g_buf, sems.at[4]))
            else:
                for j, block in enumerate(blocks):
                    there = pl.ds(pl.multiple_of(info[10 + j] * QUARTER, QUARTER), QUARTER)
                    act(pltpu.make_async_copy(block.at[:QUARTER], w_buf.at[there], sems.at[j]))
                if g_buf is not None:
                    act(pltpu.make_async_copy(blocks[0].at[QUARTER:], g_buf, sems.at[4]))


def pack_kernel(near, *refs):
    info, gains, kv_weights = refs[:3]
    section, quarter = info[14], info[10]
    low = 0 if near else 4
    targets = range(0 if near else 4, low + 4)
    outs, (terms, sems) = refs[3:-2], refs[-2:]
    copies = []
    for i, k in enumerate(targets):
        target = jnp.bitwise_xor(section, k)
        upper, role = target // 4, lax.rem(target, 4)
        if k > 0:
            rows = pl.ds(pl.multiple_of(role * COLS + quarter * QUARTER, QUARTER), QUARTER)
            copies.append(pltpu.make_async_copy(kv_weights.at[0, upper, rows], outs[i].at[:QUARTER], sems.at[i]))
            copies[-1].start()
    for i, k in enumerate(targets):
        target = jnp.bitwise_xor(section, k)
        at = pl.ds(pl.multiple_of(lax.rem(target, 4) * COLS, COLS), COLS)
        gain = jnp.where(target // 4 == 0, gains[0, 0:1, at], gains[0, 1:2, at])
        high = gain.astype(BF).astype(F32)
        middle = (gain - high).astype(BF).astype(F32)
        row = lax.broadcasted_iota(jnp.int32, (STAT, COLS), 0)
        block = jnp.where(row == 0, high, jnp.where(row == 1, middle, jnp.where(row == 2, gain - high - middle, 0.0)))
        terms[i] = block.astype(BF)
        there = outs[i] if k == 0 else outs[i].at[QUARTER:]
        copies.append(pltpu.make_async_copy(terms.at[i], there, sems.at[4 + i]))
        copies[-1].start()
    for copy in copies:
        copy.wait()


def start_copy(copy):
    copy.start()


def wait_copy(copy):
    copy.wait()


def project(h, gain, info, w_buf, flat, out):
    wide = h.astype(F32)
    flat[...] = jnp.dot((wide * gain).astype(BF), w_buf[...], preferred_element_type=F32)
    stats = split_rows(as_row(jnp.sum(wide * wide, axis=1, keepdims=True)))
    role = info[8]
    for k in range(4):
        head = jnp.bitwise_xor(role, k)
        at_key = pl.ds(pl.multiple_of(head * HEAD_DIM, HEAD_DIM), HEAD_DIM)
        at_value = pl.ds(pl.multiple_of((head + KV_HEADS) * HEAD_DIM, HEAD_DIM), HEAD_DIM)
        out[k, : 2 * ROWS, :HEAD_DIM] = flat[:, at_key].astype(BF)
        out[k, : 2 * ROWS, HEAD_DIM:] = flat[:, at_value].astype(BF)
        out[k, 2 * ROWS :, :] = stats


def add_parts(parts):
    total = parts[0].astype(F32)
    for part in parts[1:]:
        total = total + part.astype(F32)
    return total


def forward_kernel(layer, n_w, *refs):
    attend, projects = layer >= 0, layer + 1 < LAYERS
    at = 0
    info = refs[0]
    h_ref = refs[1]
    at = 2
    if attend:
        gain_ref, parts, bias_ref = refs[at], refs[at + 1 : at + 5], refs[at + 5]
        at += 6
    if projects:
        w_refs = refs[at : at + n_w]
        at += n_w
    if attend:
        h_out, state_out, kvprev_out = refs[at : at + 3]
        at += 3
    if projects:
        piece_out = refs[at]
        gain_out = refs[at + 1]
        w_buf, g_buf, flat, sems = refs[at + 2 : at + 6]
        load_weights(layer + 1, info, w_refs, w_buf, g_buf, sems, start_copy)
    h = h_ref[...]
    if attend:
        total = add_parts([p[...] for p in parts])
        ss = total[2 * ROWS : 2 * ROWS + 1] + total[2 * ROWS + 1 : 2 * ROWS + 2]
        inv = as_column(lax.rsqrt(ss * (1.0 / D) + epsilon))
        kv = (total[: 2 * ROWS] * inv).astype(BF)
        wide = h.astype(F32)
        queries = (wide * inv * gain_ref[:1]).astype(BF)
        inv_high = inv.astype(BF).astype(F32)
        inv_low = inv - inv_high
        lane = lax.broadcasted_iota(jnp.int32, (ROWS, HEAD_DIM), 1)
        state_out[:, :COLS] = h[ROWS:]
        state_out[:, COLS : COLS + 2 * HEAD_DIM] = kv[ROWS:]
        state_out[:, COLS + 2 * HEAD_DIM :] = jnp.where(
            lane < HEAD_DIM // 2, inv_high[ROWS:], inv_low[ROWS:]
        ).astype(BF)
        kvprev_out[...] = kv[:ROWS]
        keys, values = kv[:, :HEAD_DIM], kv[:, HEAD_DIM:]
        before = softmax_of(stack_heads(queries[:ROWS]), keys[:ROWS], bias_ref[0][:, ROWS:]).astype(BF)
        mixed = jnp.dot(before, values[:ROWS], preferred_element_type=F32)
        h_out[:ROWS] = (wide[:ROWS] + unstack_heads(mixed, ROWS)).astype(BF)
        own = softmax_of(stack_heads(queries[ROWS:]), keys, bias_ref[1]).astype(BF)
        mixed = jnp.dot(own, values, preferred_element_type=F32)
        h_out[ROWS:] = (wide[ROWS:] + unstack_heads(mixed, ROWS)).astype(BF)
        h = h_out[...] if projects else None
    if projects:
        load_weights(layer + 1, info, w_refs, w_buf, g_buf, sems, wait_copy)
        terms = g_buf[...].astype(F32)
        gain = terms[0:1] + terms[1:2] + terms[2:3]
        gain_out[...] = jnp.broadcast_to(gain, gain_out.shape)
        project(h, gain, info, w_buf, flat, piece_out)


def state_parts(own, following):
    h = jnp.concatenate([own[:, :COLS], following[:, :COLS]], axis=0).astype(F32)
    stat = jnp.concatenate([own[:, COLS + 2 * HEAD_DIM :], following[:, COLS + 2 * HEAD_DIM :]], axis=0)
    stat = stat.astype(F32)
    inv = stat[:, :1] + stat[:, HEAD_DIM // 2 : HEAD_DIM // 2 + 1]
    return h, inv


def attend_back(weights, cotangent, values):
    grad_weights = dot_nt(cotangent, values).astype(BF).astype(F32)
    inner = jnp.sum(weights * grad_weights, axis=1, keepdims=True)
    grad_scores = (weights * (grad_weights - inner) * SCALE).astype(BF)
    return weights.astype(BF), grad_scores


def backward_kernel(layer, n_w, *refs):
    finish, attend = layer + 1 < LAYERS, layer >= 0
    info, d_ref = refs[:2]
    at = 2
    if finish:
        gain_up, dq_ref = refs[at : at + 2]
        at += 1
        parts = refs[at + 1 : at + 5]
        up_own, up_next = refs[at + 5 : at + 7]
        w_refs = refs[at + 7 : at + 7 + n_w]
        at += 7 + n_w
    if attend:
        gain_ref, own_ref, next_ref, prev_ref, bias_ref = refs[at : at + 5]
        at += 5
    if finish:
        out_ref = refs[at]
        at += 1
    if attend:
        if finish:
            d_out = refs[at]
            at += 1
        dq_out, piece_out = refs[at : at + 2]
        at += 2
    if attend:
        soft0, soft1 = refs[-2:]
    if finish:
        w_buf, flat, sems = refs[at : at + 3]
        at += 3
        load_weights(layer + 1, info, w_refs, w_buf, None, sems, start_copy)
        role = info[8]
        stats = jnp.zeros((1, 2 * ROWS), F32)
        for k in range(4):
            head = jnp.bitwise_xor(role, k)
            at_key = pl.ds(pl.multiple_of(head * HEAD_DIM, HEAD_DIM), HEAD_DIM)
            at_value = pl.ds(pl.multiple_of((head + KV_HEADS) * HEAD_DIM, HEAD_DIM), HEAD_DIM)
            flat[:, at_key] = parts[k][: 2 * ROWS, :HEAD_DIM]
            flat[:, at_value] = parts[k][: 2 * ROWS, HEAD_DIM:]
            tail = parts[k][2 * ROWS :, :].astype(F32)
            stats = stats + tail[0:1] + tail[1:2]
        shift = as_column(stats * (1.0 / D))
    if attend:
        below, below_inv = state_parts(own_ref, next_ref)
        queries = (below * below_inv * gain_ref[:1]).astype(BF)
        kv_own = own_ref[:, COLS : COLS + 2 * HEAD_DIM]
        kv_next = next_ref[:, COLS : COLS + 2 * HEAD_DIM]
        kv0 = jnp.concatenate([prev_ref[...], kv_own], axis=0)
        kv1 = jnp.concatenate([kv_own, kv_next], axis=0)
        q0, q1 = stack_heads(queries[:ROWS]), stack_heads(queries[ROWS:])
        soft0[...] = softmax_of(q0, kv0[:, :HEAD_DIM], bias_ref[1])
        soft1[...] = softmax_of(q1, kv1[:, :HEAD_DIM], bias_ref[2])
    if finish:
        h, inv = state_parts(up_own, up_next)
        base = d_ref[...].astype(F32) - h * (inv * inv * shift)
        base_gain = gain_up[:1]
        load_weights(layer + 1, info, w_refs, w_buf, None, sems, wait_copy)
        grad = dot_nt(flat[...], w_buf[...]) + dq_ref[...].astype(F32)
        d = (base + grad * base_gain * inv).astype(BF)
        out_ref[:, :COLS] = d[:ROWS]
        out_ref[:, COLS:] = parts[0][:ROWS, :]
        if attend:
            d_out[...] = d
    else:
        d = d_ref[...]
    if attend:
        d0 = stack_heads(d[:ROWS])
        w0, s0 = attend_back(soft0[...], d0, kv0[:, HEAD_DIM:])
        dq0 = unstack_heads(jnp.dot(s0, kv0[:, :HEAD_DIM], preferred_element_type=F32), ROWS).astype(BF)
        dk_own = dot_tn(s0[:, ROWS:], q0)
        dv_own = dot_tn(w0[:, ROWS:], d0)
        d1 = stack_heads(d[ROWS:])
        w1, s1 = attend_back(soft1[...], d1, kv1[:, HEAD_DIM:])
        dq1 = unstack_heads(jnp.dot(s1, kv1[:, :HEAD_DIM], preferred_element_type=F32), ROWS).astype(BF)
        dk = dot_tn(s1, q1)
        dv = dot_tn(w1, d1)
        dkv_own = jnp.concatenate([dk_own + dk[:ROWS], dv_own + dv[:ROWS]], axis=1).astype(BF)
        dkv_next = jnp.concatenate([dk[ROWS:], dv[ROWS:]], axis=1).astype(BF)
        dq_out[:ROWS] = dq0
        dq_out[ROWS:] = dq1
        dkv = jnp.concatenate([dkv_own, dkv_next], axis=0)
        dq = jnp.concatenate([dq0, dq1], axis=0)
        column = jnp.sum(dq.astype(F32) * queries.astype(F32), axis=1, keepdims=True)
        column = column + jnp.sum(dkv.astype(F32) * kv1.astype(F32), axis=1, keepdims=True)
        piece_out[: 2 * ROWS, :] = dkv
        piece_out[2 * ROWS :, :] = split_rows(as_row(column))


SMEM_SPEC = pl.BlockSpec(memory_space=pltpu.SMEM)
VMEM_SPEC = pl.BlockSpec(memory_space=pltpu.VMEM)
GAIN = (8, COLS)
ANY_SPEC = pl.BlockSpec(memory_space=pltpu.HBM)


def call(kernel, operands, specs, outs, scratch, flops):
    return pl.pallas_call(
        kernel,
        out_shape=[jax.ShapeDtypeStruct(shape, F32 if shape == GAIN else BF) for shape in outs],
        in_specs=specs,
        out_specs=[VMEM_SPEC] * len(outs),
        scratch_shapes=scratch,
        compiler_params=pltpu.CompilerParams(vmem_limit_bytes=VMEM_LIMIT),
        cost_estimate=pl.CostEstimate(flops=flops, bytes_accessed=4 << 20, transcendentals=0),
    )(*operands)


def pack_call(near, info, gains, kv_weights):
    message = (QUARTER + STAT, WIDTH)
    outs = [(STAT, COLS)] + [message] * 3 if near else [message] * 4
    return pl.pallas_call(
        functools.partial(pack_kernel, near),
        out_shape=[jax.ShapeDtypeStruct(shape, BF) for shape in outs],
        in_specs=[SMEM_SPEC, VMEM_SPEC] + [ANY_SPEC],
        out_specs=[VMEM_SPEC] * len(outs),
        scratch_shapes=[pltpu.VMEM((4, STAT, COLS), BF), pltpu.SemaphoreType.DMA((8,))],
        compiler_params=pltpu.CompilerParams(vmem_limit_bytes=VMEM_LIMIT),
        cost_estimate=pl.CostEstimate(flops=0, bytes_accessed=4 << 20, transcendentals=0),
    )(info, gains, kv_weights)


def after(block, dependency):
    return lax.optimization_barrier((block, dependency))[0]


def forward_call(layer, info, h, gain, parts, bias, weights):
    attend, projects = layer >= 0, layer + 1 < LAYERS
    operands, specs = [info, h], [SMEM_SPEC, VMEM_SPEC]
    outs, scratch, n_w = [], [], 0
    if attend:
        operands += [gain] + list(parts) + [bias]
        specs += [VMEM_SPEC] * 6
        outs += [(2 * ROWS, COLS), (ROWS, STATE), (ROWS, 2 * HEAD_DIM)]
    if projects:
        w_refs = weights[(layer + 1) // 4]
        n_w = len(w_refs)
        operands += w_refs
        specs += [ANY_SPEC] * n_w
        outs += [(4, 2 * ROWS + STAT, 2 * HEAD_DIM), GAIN]
        scratch = [
            pltpu.VMEM((COLS, WIDTH), BF),
            pltpu.VMEM((STAT, COLS), BF),
            pltpu.VMEM((2 * ROWS, WIDTH), F32),
            pltpu.SemaphoreType.DMA((5,)),
        ]
    return call(functools.partial(forward_kernel, layer, n_w), operands, specs, outs, scratch, 2 << 30)


def backward_call(layer, info, d, gains, dq, parts, up, here, kvprev, bias, weights):
    finish, attend = layer + 1 < LAYERS, layer >= 0
    operands, specs = [info, d], [SMEM_SPEC, VMEM_SPEC]
    outs, scratch, n_w = [], [], 0
    if finish:
        w_refs = weights[(layer + 1) // 4]
        n_w = len(w_refs)
        operands += [gains[layer + 1], dq] + list(parts) + list(up) + w_refs
        specs += [VMEM_SPEC] * 8 + [ANY_SPEC] * n_w
        outs += [(ROWS, COLS + 2 * HEAD_DIM)]
        scratch = [
            pltpu.VMEM((COLS, WIDTH), BF),
            pltpu.VMEM((2 * ROWS, WIDTH), BF),
            pltpu.SemaphoreType.DMA((5,)),
        ]
    if attend:
        operands += [gains[layer]] + list(here) + [kvprev, bias]
        specs += [VMEM_SPEC] * 5
        if finish:
            outs += [(2 * ROWS, COLS)]
        outs += [(2 * ROWS, COLS), (2 * ROWS + STAT, 2 * HEAD_DIM)]
        scratch += [pltpu.VMEM((GROUP * ROWS, 2 * ROWS), F32)] * 2
    return call(functools.partial(backward_kernel, layer, n_w), operands, specs, outs, scratch, 4 << 30)


def pick(blocks, index):
    return lax.select_n(index, *blocks)


def deliver(messages, section, low):
    upper = section // 4
    here = lax.rem(section, 4)
    got = []
    for k in range(4):
        target = jnp.bitwise_xor(section, k + low)
        layer = jnp.where(upper == 0, target, LAYERS - 1 - target) - low
        block = pick(messages, layer)
        got.append(block if k + low == 0 else send(block, to_section(k + low)))
    return [pick(got, jnp.bitwise_xor(here, role)) for role in range(4)]


def per_device(x_a, x_b, grad_a, grad_b, gains, kv_weights, doc_lengths):
    section = lax.axis_index("section").astype(jnp.int32)
    shard = lax.axis_index("seq").astype(jnp.int32)
    upper = section // 4
    role = lax.rem(section, 4)
    core = lax.rem(shard, 2)
    first = upper == 0

    parity = lax.rem(shard // 2, 2)

    layers = jnp.arange(LAYERS, dtype=jnp.int32)
    holders = jnp.where(first, layers, LAYERS - 1 - layers)
    quarter = 2 * parity + core
    arrival = jnp.stack([quarter, jnp.bitwise_xor(quarter, 2), jnp.bitwise_xor(quarter, 1), 3 - quarter])
    info = jnp.concatenate([jnp.bitwise_xor(section, holders), jnp.stack([role, upper]), arrival, section[None], jnp.zeros((1,), jnp.int32)])

    def spread(mine):
        beside = send(mine, to_beside())
        return [mine, beside, send(mine, to_mate()), send(beside, to_mate())]

    own_gain, *near = pack_call(True, info, gains, kv_weights)
    columns = role * COLS
    x_own = lax.dynamic_slice(jnp.where(first, x_a, x_b), (0, columns), (ROWS, COLS))
    near = [send(near[k - 1], to_section(k)) for k in range(1, 4)]
    far = pack_call(False, after(info, near[0]), gains, kv_weights)
    weights = [[kv_weights, own_gain] + [w for block in near for w in spread(block)], []]

    far_blocks = {}

    def send_far(i, block):
        far_blocks[i] = spread(send(block, to_section(4 + i, flip=True)))

    lengths = jnp.where(first, doc_lengths[0], doc_lengths[1])
    which = jnp.arange(lengths.shape[0])
    ends = jnp.sum(jnp.where(which[None, :] <= which[:, None], lengths[None, :], 0), axis=1)
    places = (shard - 2) * ROWS + jnp.arange(4 * ROWS, dtype=jnp.int32)
    docs = jnp.sum((ends[None, :] <= places[:, None]).astype(jnp.int32), axis=1)
    docs = jnp.where(places < 0, -1, docs)
    bias = []
    for block in range(3):
        q_place, q_doc = places[(block + 1) * ROWS : (block + 2) * ROWS], docs[(block + 1) * ROWS : (block + 2) * ROWS]
        k_place, k_doc = places[block * ROWS : (block + 2) * ROWS], docs[block * ROWS : (block + 2) * ROWS]
        allowed = (q_doc[:, None] == k_doc[None, :]) & (k_place[None, :] <= q_place[:, None])
        bias.append(jnp.where(allowed, 0.0, -1e30).astype(F32))
    bias = jnp.stack(bias)

    h = jnp.concatenate([send(x_own, to_shard(1)), x_own], axis=0)

    def exchange(pieces):
        return [pieces[0]] + [send(pieces[k], to_section(k)) for k in range(1, 4)]

    send_far(1, after(far[1], near[1]))
    send_far(3, after(far[3], near[1]))
    pieces, gain = forward_call(-1, info, h, None, None, bias, weights)
    states, befores, acts, gain_rows = [], [], [], [gain]
    for layer in range(LAYERS):
        parts = exchange([pieces[k] for k in range(4)])
        if layer == 0:
            send_far(2, after(far[2], parts[3]))
            send_far(0, after(far[0], parts[3]))
            weights[1] += [w for i in range(4) for w in far_blocks[i]]
        if layer == 1:
            start = after(columns, parts[3])
            grad_own = lax.dynamic_slice(jnp.where(first, grad_a, grad_b), (0, start), (ROWS, COLS))
            cotangent = jnp.concatenate([grad_own, send(grad_own, to_shard(-1))], axis=0)
        out = forward_call(layer, info, h, gain_rows[layer], parts, bias, weights)
        h, state, before = out[:3]
        if layer + 1 < LAYERS:
            pieces = out[3]
            gain_rows.append(out[4])
        states.append((state, send(state, to_shard(-1))))
        befores.append(before)
        acts.append(h[ROWS:])

    act_sets = [deliver(acts[:4], section, 0), deliver(acts[4:], section, 4)]

    d = cotangent
    dq, piece = backward_call(
        LAYERS - 1, info, d, gain_rows, None, None, None, states[-1], befores[-1], bias, weights
    )
    grads = [None] * LAYERS
    for layer in range(LAYERS - 2, -2, -1):
        parts = exchange([piece] * 4)
        here = states[layer] if layer >= 0 else None
        before = befores[layer] if layer >= 0 else None
        out = backward_call(
            layer, info, d, gain_rows, dq, parts, states[layer + 1], here, before, bias, weights
        )
        grads[layer + 1] = out[0]
        if layer >= 0:
            d, dq, piece = out[1:]
    grad_sets = [deliver(grads[:4], section, 0), deliver(grads[4:], section, 4)]

    def assemble(sets, cut):
        near = jnp.concatenate([cut(b) for b in sets[0]], axis=1)
        far = jnp.concatenate([cut(b) for b in sets[1]], axis=1)
        return jnp.stack([jnp.where(first, near, far), jnp.where(first, far, near)])[:, None]

    acts_out = assemble(act_sets, lambda b: b)
    ingrad_out = assemble(grad_sets, lambda b: b[:, :COLS])
    keys = assemble(grad_sets, lambda b: b[:, COLS : COLS + HEAD_DIM])
    values = assemble(grad_sets, lambda b: b[:, COLS + HEAD_DIM :])
    return acts_out, ingrad_out, jnp.concatenate([keys, values], axis=-1)


def solution(mesh):
    in_specs = (
        P("seq", None),
        P("seq", None),
        P("seq", None),
        P("seq", None),
        P("section", None, None),
        P("section", None, None, None),
        P(),
    )
    out_specs = (
        P(None, "section", "seq", None),
        P(None, "section", "seq", None),
        P(None, "section", "seq", None),
    )
    return jax.shard_map(
        per_device, mesh=mesh, in_specs=in_specs, out_specs=out_specs, check_vma=False
    )
```

```python
import functools
import math

import jax
import jax.numpy as jnp
from jax import lax
from jax.experimental import pallas as pl
from jax.experimental.pallas import tpu as pltpu
from jax.sharding import PartitionSpec as P

HEADS = 32
HEAD_DIM = 128
KV_HEADS = 4
LAYERS = 8
GROUP = HEADS // KV_HEADS
ROWS = 128
COLS = GROUP * HEAD_DIM
WIDTH = 2 * KV_HEADS * HEAD_DIM
D = HEADS * HEAD_DIM
QUARTER = COLS // 4
STAT = 16
STATE = COLS + 3 * HEAD_DIM
SCALE = 1.0 / math.sqrt(HEAD_DIM)
epsilon = 1e-05

BF = jnp.bfloat16
F32 = jnp.float32
AXES = ("section", "seq")
VMEM_LIMIT = 48 * 1024 * 1024


def route(target):
    pairs = []
    for section in range(8):
        for shard in range(16):
            there = target(section, shard)
            pairs.append((section * 16 + shard, there[0] * 16 + there[1]))
    return pairs


def to_section(k, flip=False):
    return route(lambda s, q: (s ^ k, q ^ (8 if flip and q & 1 else 0)))


def to_shard(step):
    return route(lambda s, q: (s, (q + step) % 16))


def to_mate():
    return route(lambda s, q: (s, q ^ 1))


def to_beside():
    return route(lambda s, q: (s, q ^ (6 if q & 1 else 2)))


def send(block, pairs):
    return lax.ppermute(block, AXES, pairs)


def eye_mask(n):
    return lax.broadcasted_iota(jnp.int32, (n, n), 0) == lax.broadcasted_iota(jnp.int32, (n, n), 1)


def as_row(column):
    n = column.shape[0]
    return jnp.sum(jnp.where(eye_mask(n), column, 0.0), axis=0, keepdims=True)


def as_column(row):
    n = row.shape[1]
    return jnp.sum(jnp.where(eye_mask(n), row, 0.0), axis=1, keepdims=True)


def split_rows(row):
    high = row.astype(BF).astype(F32)
    low = row - high
    at = lax.broadcasted_iota(jnp.int32, (STAT, row.shape[1]), 0)
    return jnp.where(at == 0, high, jnp.where(at == 1, low, 0.0)).astype(BF)


def stack_heads(block):
    return jnp.concatenate([block[:, i * HEAD_DIM : (i + 1) * HEAD_DIM] for i in range(GROUP)], axis=0)


def turn_heads(block):
    return jnp.concatenate([block[:, i * ROWS : (i + 1) * ROWS].T for i in range(GROUP)], axis=1)


def dot(a, b):
    return jnp.dot(a, b, preferred_element_type=F32)


def dot_nt(a, b):
    return lax.dot_general(a, b, (((1,), (1,)), ((), ())), preferred_element_type=F32)


def dot_tn(a, b):
    return lax.dot_general(a, b, (((0,), (0,)), ((), ())), preferred_element_type=F32)


def softmax_of(queries, keys, bias):
    scores = dot_nt(keys, queries) * SCALE + jnp.concatenate([bias] * GROUP, axis=1)
    powers = jnp.exp(scores - jnp.max(scores, axis=0, keepdims=True))
    return powers * (1.0 / jnp.sum(powers, axis=0, keepdims=True))


def load_weights(layer, info, w_refs, w_buf, g_buf, sems, act):
    low = layer < LAYERS // 2
    k_here, role, direction = info[layer], info[8], info[9]
    for k in range(4):
        blocks = w_refs[4 * (k - 1) + 2 : 4 * (k - 1) + 6] if low else w_refs[4 * k : 4 * k + 4]

        @pl.when(k_here == (k if low else k + 4))
        def _():
            if low and k == 0:
                rows = pl.ds(pl.multiple_of(role * COLS, COLS), COLS)
                act(pltpu.make_async_copy(w_refs[0].at[0, direction, rows], w_buf, sems.at[0]))
                if g_buf is not None:
                    act(pltpu.make_async_copy(w_refs[1], g_buf, sems.at[4]))
            else:
                for j, block in enumerate(blocks):
                    there = pl.ds(pl.multiple_of(info[10 + j] * QUARTER, QUARTER), QUARTER)
                    act(pltpu.make_async_copy(block.at[:QUARTER], w_buf.at[there], sems.at[j]))
                if g_buf is not None:
                    act(pltpu.make_async_copy(blocks[0].at[QUARTER:], g_buf, sems.at[4]))


def pack_kernel(near, *refs):
    info, gains, kv_weights = refs[:3]
    section, quarter = info[14], info[10]
    low = 0 if near else 4
    targets = range(0 if near else 4, low + 4)
    outs, (terms, sems) = refs[3:-2], refs[-2:]
    copies = []
    for i, k in enumerate(targets):
        target = jnp.bitwise_xor(section, k)
        upper, role = target // 4, lax.rem(target, 4)
        if k > 0:
            rows = pl.ds(pl.multiple_of(role * COLS + quarter * QUARTER, QUARTER), QUARTER)
            copies.append(pltpu.make_async_copy(kv_weights.at[0, upper, rows], outs[i].at[:QUARTER], sems.at[i]))
            copies[-1].start()
    for i, k in enumerate(targets):
        target = jnp.bitwise_xor(section, k)
        at = pl.ds(pl.multiple_of(lax.rem(target, 4) * COLS, COLS), COLS)
        gain = jnp.where(target // 4 == 0, gains[0, 0:1, at], gains[0, 1:2, at])
        high = gain.astype(BF).astype(F32)
        middle = (gain - high).astype(BF).astype(F32)
        row = lax.broadcasted_iota(jnp.int32, (STAT, COLS), 0)
        block = jnp.where(row == 0, high, jnp.where(row == 1, middle, jnp.where(row == 2, gain - high - middle, 0.0)))
        terms[i] = block.astype(BF)
        there = outs[i] if k == 0 else outs[i].at[QUARTER:]
        copies.append(pltpu.make_async_copy(terms.at[i], there, sems.at[4 + i]))
        copies[-1].start()
    for copy in copies:
        copy.wait()


def start_copy(copy):
    copy.start()


def wait_copy(copy):
    copy.wait()


def project(h, gain, info, w_buf, flat, out):
    wide = h.astype(F32)
    flat[...] = jnp.dot((wide * gain).astype(BF), w_buf[...], preferred_element_type=F32)
    stats = split_rows(as_row(jnp.sum(wide * wide, axis=1, keepdims=True)))
    role = info[8]
    for k in range(4):
        head = jnp.bitwise_xor(role, k)
        at_key = pl.ds(pl.multiple_of(head * HEAD_DIM, HEAD_DIM), HEAD_DIM)
        at_value = pl.ds(pl.multiple_of((head + KV_HEADS) * HEAD_DIM, HEAD_DIM), HEAD_DIM)
        out[k, : 2 * ROWS, :HEAD_DIM] = flat[:, at_key].astype(BF)
        out[k, : 2 * ROWS, HEAD_DIM:] = flat[:, at_value].astype(BF)
        out[k, 2 * ROWS :, :] = stats


def add_parts(parts):
    total = parts[0].astype(F32)
    for part in parts[1:]:
        total = total + part.astype(F32)
    return total


def forward_kernel(layer, n_w, *refs):
    attend, projects = layer >= 0, layer + 1 < LAYERS
    at = 0
    info = refs[0]
    h_ref = refs[1]
    at = 2
    if attend:
        gain_ref, parts, bias_ref = refs[at], refs[at + 1 : at + 5], refs[at + 5]
        at += 6
    if projects:
        w_refs = refs[at : at + n_w]
        at += n_w
    if attend:
        h_out, state_out, kvprev_out = refs[at : at + 3]
        at += 3
    if projects:
        piece_out = refs[at]
        gain_out = refs[at + 1]
        w_buf, g_buf, flat, sems = refs[at + 2 : at + 6]
        load_weights(layer + 1, info, w_refs, w_buf, g_buf, sems, start_copy)
    h = h_ref[...]
    if attend:
        total = add_parts([p[...] for p in parts])
        ss = total[2 * ROWS : 2 * ROWS + 1] + total[2 * ROWS + 1 : 2 * ROWS + 2]
        inv = as_column(lax.rsqrt(ss * (1.0 / D) + epsilon))
        kv = (total[: 2 * ROWS] * inv).astype(BF)
        wide = h.astype(F32)
        queries = (wide * inv * gain_ref[:1]).astype(BF)
        inv_high = inv.astype(BF).astype(F32)
        inv_low = inv - inv_high
        lane = lax.broadcasted_iota(jnp.int32, (ROWS, HEAD_DIM), 1)
        state_out[:, :COLS] = h[ROWS:]
        state_out[:, COLS : COLS + 2 * HEAD_DIM] = kv[ROWS:]
        state_out[:, COLS + 2 * HEAD_DIM :] = jnp.where(
            lane < HEAD_DIM // 2, inv_high[ROWS:], inv_low[ROWS:]
        ).astype(BF)
        kvprev_out[...] = kv[:ROWS]
        keys, values = kv[:, :HEAD_DIM], kv[:, HEAD_DIM:]
        before = softmax_of(stack_heads(queries[:ROWS]), keys[:ROWS], bias_ref[0][ROWS:]).astype(BF)
        h_out[:ROWS] = (wide[:ROWS] + turn_heads(dot_tn(values[:ROWS], before))).astype(BF)
        own = softmax_of(stack_heads(queries[ROWS:]), keys, bias_ref[1]).astype(BF)
        h_out[ROWS:] = (wide[ROWS:] + turn_heads(dot_tn(values, own))).astype(BF)
        h = h_out[...] if projects else None
    if projects:
        load_weights(layer + 1, info, w_refs, w_buf, g_buf, sems, wait_copy)
        terms = g_buf[...].astype(F32)
        gain = terms[0:1] + terms[1:2] + terms[2:3]
        gain_out[...] = jnp.broadcast_to(gain, gain_out.shape)
        project(h, gain, info, w_buf, flat, piece_out)


def state_parts(own, following):
    h = jnp.concatenate([own[:, :COLS], following[:, :COLS]], axis=0).astype(F32)
    stat = jnp.concatenate([own[:, COLS + 2 * HEAD_DIM :], following[:, COLS + 2 * HEAD_DIM :]], axis=0)
    stat = stat.astype(F32)
    inv = stat[:, :1] + stat[:, HEAD_DIM // 2 : HEAD_DIM // 2 + 1]
    return h, inv


def attend_back(weights, cotangent, values):
    grad_weights = dot_nt(values, cotangent).astype(BF).astype(F32)
    inner = jnp.sum(weights * grad_weights, axis=0, keepdims=True)
    grad_scores = (weights * (grad_weights - inner) * SCALE).astype(BF)
    return weights.astype(BF), grad_scores


def backward_kernel(layer, n_w, *refs):
    finish, attend = layer + 1 < LAYERS, layer >= 0
    info, d_ref = refs[:2]
    at = 2
    if finish:
        gain_up, dq_ref = refs[at : at + 2]
        at += 1
        parts = refs[at + 1 : at + 5]
        up_own, up_next = refs[at + 5 : at + 7]
        w_refs = refs[at + 7 : at + 7 + n_w]
        at += 7 + n_w
    if attend:
        gain_ref, own_ref, next_ref, prev_ref, bias_ref = refs[at : at + 5]
        at += 5
    if finish:
        out_ref = refs[at]
        at += 1
    if attend:
        if finish:
            d_out = refs[at]
            at += 1
        dq_out, piece_out = refs[at : at + 2]
        at += 2
    if attend:
        soft0, soft1 = refs[-2:]
    if finish:
        w_buf, flat, sems = refs[at : at + 3]
        at += 3
        load_weights(layer + 1, info, w_refs, w_buf, None, sems, start_copy)
        role = info[8]
        stats = jnp.zeros((1, 2 * ROWS), F32)
        for k in range(4):
            head = jnp.bitwise_xor(role, k)
            at_key = pl.ds(pl.multiple_of(head * HEAD_DIM, HEAD_DIM), HEAD_DIM)
            at_value = pl.ds(pl.multiple_of((head + KV_HEADS) * HEAD_DIM, HEAD_DIM), HEAD_DIM)
            flat[:, at_key] = parts[k][: 2 * ROWS, :HEAD_DIM]
            flat[:, at_value] = parts[k][: 2 * ROWS, HEAD_DIM:]
            tail = parts[k][2 * ROWS :, :].astype(F32)
            stats = stats + tail[0:1] + tail[1:2]
        shift = as_column(stats * (1.0 / D))
    if attend:
        below, below_inv = state_parts(own_ref, next_ref)
        queries = (below * below_inv * gain_ref[:1]).astype(BF)
        kv_own = own_ref[:, COLS : COLS + 2 * HEAD_DIM]
        kv_next = next_ref[:, COLS : COLS + 2 * HEAD_DIM]
        kv0 = jnp.concatenate([prev_ref[...], kv_own], axis=0)
        kv1 = jnp.concatenate([kv_own, kv_next], axis=0)
        q0, q1 = stack_heads(queries[:ROWS]), stack_heads(queries[ROWS:])
        soft0[...] = softmax_of(q0, kv0[:, :HEAD_DIM], bias_ref[1])
        soft1[...] = softmax_of(q1, kv1[:, :HEAD_DIM], bias_ref[2])
    if finish:
        h, inv = state_parts(up_own, up_next)
        base = d_ref[...].astype(F32) - h * (inv * inv * shift)
        base_gain = gain_up[:1]
        load_weights(layer + 1, info, w_refs, w_buf, None, sems, wait_copy)
        grad = dot_nt(flat[...], w_buf[...]) + dq_ref[...].astype(F32)
        d = (base + grad * base_gain * inv).astype(BF)
        out_ref[:, :COLS] = d[:ROWS]
        out_ref[:, COLS:] = parts[0][:ROWS, :]
        if attend:
            d_out[...] = d
    else:
        d = d_ref[...]
    if attend:
        d0 = stack_heads(d[:ROWS])
        w0, s0 = attend_back(soft0[...], d0, kv0[:, HEAD_DIM:])
        dq0 = turn_heads(dot_tn(kv0[:, :HEAD_DIM], s0)).astype(BF)
        dk_own = dot(s0[ROWS:], q0)
        dv_own = dot(w0[ROWS:], d0)
        d1 = stack_heads(d[ROWS:])
        w1, s1 = attend_back(soft1[...], d1, kv1[:, HEAD_DIM:])
        dq1 = turn_heads(dot_tn(kv1[:, :HEAD_DIM], s1)).astype(BF)
        dk = dot(s1, q1)
        dv = dot(w1, d1)
        dkv_own = jnp.concatenate([dk_own + dk[:ROWS], dv_own + dv[:ROWS]], axis=1).astype(BF)
        dkv_next = jnp.concatenate([dk[ROWS:], dv[ROWS:]], axis=1).astype(BF)
        dq_out[:ROWS] = dq0
        dq_out[ROWS:] = dq1
        dkv = jnp.concatenate([dkv_own, dkv_next], axis=0)
        dq = jnp.concatenate([dq0, dq1], axis=0)
        column = jnp.sum(dq.astype(F32) * queries.astype(F32), axis=1, keepdims=True)
        column = column + jnp.sum(dkv.astype(F32) * kv1.astype(F32), axis=1, keepdims=True)
        piece_out[: 2 * ROWS, :] = dkv
        piece_out[2 * ROWS :, :] = split_rows(as_row(column))


SMEM_SPEC = pl.BlockSpec(memory_space=pltpu.SMEM)
VMEM_SPEC = pl.BlockSpec(memory_space=pltpu.VMEM)
GAIN = (8, COLS)
ANY_SPEC = pl.BlockSpec(memory_space=pltpu.HBM)


def call(kernel, operands, specs, outs, scratch, flops):
    return pl.pallas_call(
        kernel,
        out_shape=[jax.ShapeDtypeStruct(shape, F32 if shape == GAIN else BF) for shape in outs],
        in_specs=specs,
        out_specs=[VMEM_SPEC] * len(outs),
        scratch_shapes=scratch,
        compiler_params=pltpu.CompilerParams(vmem_limit_bytes=VMEM_LIMIT),
        cost_estimate=pl.CostEstimate(flops=flops, bytes_accessed=4 << 20, transcendentals=0),
    )(*operands)


def pack_call(near, info, gains, kv_weights):
    message = (QUARTER + STAT, WIDTH)
    outs = [(STAT, COLS)] + [message] * 3 if near else [message] * 4
    return pl.pallas_call(
        functools.partial(pack_kernel, near),
        out_shape=[jax.ShapeDtypeStruct(shape, BF) for shape in outs],
        in_specs=[SMEM_SPEC, VMEM_SPEC] + [ANY_SPEC],
        out_specs=[VMEM_SPEC] * len(outs),
        scratch_shapes=[pltpu.VMEM((4, STAT, COLS), BF), pltpu.SemaphoreType.DMA((8,))],
        compiler_params=pltpu.CompilerParams(vmem_limit_bytes=VMEM_LIMIT),
        cost_estimate=pl.CostEstimate(flops=0, bytes_accessed=4 << 20, transcendentals=0),
    )(info, gains, kv_weights)


def after(block, dependency):
    return lax.optimization_barrier((block, dependency))[0]


def forward_call(layer, info, h, gain, parts, bias, weights):
    attend, projects = layer >= 0, layer + 1 < LAYERS
    operands, specs = [info, h], [SMEM_SPEC, VMEM_SPEC]
    outs, scratch, n_w = [], [], 0
    if attend:
        operands += [gain] + list(parts) + [bias]
        specs += [VMEM_SPEC] * 6
        outs += [(2 * ROWS, COLS), (ROWS, STATE), (ROWS, 2 * HEAD_DIM)]
    if projects:
        w_refs = weights[(layer + 1) // 4]
        n_w = len(w_refs)
        operands += w_refs
        specs += [ANY_SPEC] * n_w
        outs += [(4, 2 * ROWS + STAT, 2 * HEAD_DIM), GAIN]
        scratch = [
            pltpu.VMEM((COLS, WIDTH), BF),
            pltpu.VMEM((STAT, COLS), BF),
            pltpu.VMEM((2 * ROWS, WIDTH), F32),
            pltpu.SemaphoreType.DMA((5,)),
        ]
    return call(functools.partial(forward_kernel, layer, n_w), operands, specs, outs, scratch, 2 << 30)


def backward_call(layer, info, d, gains, dq, parts, up, here, kvprev, bias, weights):
    finish, attend = layer + 1 < LAYERS, layer >= 0
    operands, specs = [info, d], [SMEM_SPEC, VMEM_SPEC]
    outs, scratch, n_w = [], [], 0
    if finish:
        w_refs = weights[(layer + 1) // 4]
        n_w = len(w_refs)
        operands += [gains[layer + 1], dq] + list(parts) + list(up) + w_refs
        specs += [VMEM_SPEC] * 8 + [ANY_SPEC] * n_w
        outs += [(ROWS, COLS + 2 * HEAD_DIM)]
        scratch = [
            pltpu.VMEM((COLS, WIDTH), BF),
            pltpu.VMEM((2 * ROWS, WIDTH), BF),
            pltpu.SemaphoreType.DMA((5,)),
        ]
    if attend:
        operands += [gains[layer]] + list(here) + [kvprev, bias]
        specs += [VMEM_SPEC] * 5
        if finish:
            outs += [(2 * ROWS, COLS)]
        outs += [(2 * ROWS, COLS), (2 * ROWS + STAT, 2 * HEAD_DIM)]
        scratch += [pltpu.VMEM((2 * ROWS, GROUP * ROWS), F32)] * 2
    return call(functools.partial(backward_kernel, layer, n_w), operands, specs, outs, scratch, 4 << 30)


def pick(blocks, index):
    return lax.select_n(index, *blocks)


def deliver(messages, section, low):
    upper = section // 4
    here = lax.rem(section, 4)
    got = []
    for k in range(4):
        target = jnp.bitwise_xor(section, k + low)
        layer = jnp.where(upper == 0, target, LAYERS - 1 - target) - low
        block = pick(messages, layer)
        got.append(block if k + low == 0 else send(block, to_section(k + low)))
    return [pick(got, jnp.bitwise_xor(here, role)) for role in range(4)]


def per_device(x_a, x_b, grad_a, grad_b, gains, kv_weights, doc_lengths):
    section = lax.axis_index("section").astype(jnp.int32)
    shard = lax.axis_index("seq").astype(jnp.int32)
    upper = section // 4
    role = lax.rem(section, 4)
    core = lax.rem(shard, 2)
    first = upper == 0

    parity = lax.rem(shard // 2, 2)

    layers = jnp.arange(LAYERS, dtype=jnp.int32)
    holders = jnp.where(first, layers, LAYERS - 1 - layers)
    quarter = 2 * parity + core
    arrival = jnp.stack([quarter, jnp.bitwise_xor(quarter, 2), jnp.bitwise_xor(quarter, 1), 3 - quarter])
    info = jnp.concatenate([jnp.bitwise_xor(section, holders), jnp.stack([role, upper]), arrival, section[None], jnp.zeros((1,), jnp.int32)])

    def spread(mine):
        beside = send(mine, to_beside())
        return [mine, beside, send(mine, to_mate()), send(beside, to_mate())]

    own_gain, *near = pack_call(True, info, gains, kv_weights)
    columns = role * COLS
    x_own = lax.dynamic_slice(jnp.where(first, x_a, x_b), (0, columns), (ROWS, COLS))
    near = [send(near[k - 1], to_section(k)) for k in range(1, 4)]
    far = pack_call(False, after(info, near[0]), gains, kv_weights)
    weights = [[kv_weights, own_gain] + [w for block in near for w in spread(block)], []]

    far_blocks = {}

    def send_far(i, block):
        far_blocks[i] = spread(send(block, to_section(4 + i, flip=True)))

    lengths = jnp.where(first, doc_lengths[0], doc_lengths[1])
    which = jnp.arange(lengths.shape[0])
    ends = jnp.sum(jnp.where(which[None, :] <= which[:, None], lengths[None, :], 0), axis=1)
    places = (shard - 2) * ROWS + jnp.arange(4 * ROWS, dtype=jnp.int32)
    docs = jnp.sum((ends[None, :] <= places[:, None]).astype(jnp.int32), axis=1)
    docs = jnp.where(places < 0, -1, docs)
    bias = []
    for block in range(3):
        q_place, q_doc = places[(block + 1) * ROWS : (block + 2) * ROWS], docs[(block + 1) * ROWS : (block + 2) * ROWS]
        k_place, k_doc = places[block * ROWS : (block + 2) * ROWS], docs[block * ROWS : (block + 2) * ROWS]
        allowed = (k_doc[:, None] == q_doc[None, :]) & (k_place[:, None] <= q_place[None, :])
        bias.append(jnp.where(allowed, 0.0, -1e30).astype(F32))
    bias = jnp.stack(bias)

    h = jnp.concatenate([send(x_own, to_shard(1)), x_own], axis=0)

    def exchange(pieces):
        return [pieces[0]] + [send(pieces[k], to_section(k)) for k in range(1, 4)]

    send_far(1, after(far[1], near[1]))
    send_far(3, after(far[3], near[1]))
    pieces, gain = forward_call(-1, info, h, None, None, bias, weights)
    states, befores, acts, gain_rows = [], [], [], [gain]
    for layer in range(LAYERS):
        parts = exchange([pieces[k] for k in range(4)])
        if layer == 0:
            send_far(2, after(far[2], parts[3]))
            send_far(0, after(far[0], parts[3]))
            weights[1] += [w for i in range(4) for w in far_blocks[i]]
        if layer == 1:
            start = after(columns, parts[3])
            grad_own = lax.dynamic_slice(jnp.where(first, grad_a, grad_b), (0, start), (ROWS, COLS))
            cotangent = jnp.concatenate([grad_own, send(grad_own, to_shard(-1))], axis=0)
        out = forward_call(layer, info, h, gain_rows[layer], parts, bias, weights)
        h, state, before = out[:3]
        if layer + 1 < LAYERS:
            pieces = out[3]
            gain_rows.append(out[4])
        states.append((state, send(state, to_shard(-1))))
        befores.append(before)
        acts.append(h[ROWS:])

    act_sets = [deliver(acts[:4], section, 0), deliver(acts[4:], section, 4)]

    d = cotangent
    dq, piece = backward_call(
        LAYERS - 1, info, d, gain_rows, None, None, None, states[-1], befores[-1], bias, weights
    )
    grads = [None] * LAYERS
    for layer in range(LAYERS - 2, -2, -1):
        parts = exchange([piece] * 4)
        here = states[layer] if layer >= 0 else None
        before = befores[layer] if layer >= 0 else None
        out = backward_call(
            layer, info, d, gain_rows, dq, parts, states[layer + 1], here, before, bias, weights
        )
        grads[layer + 1] = out[0]
        if layer >= 0:
            d, dq, piece = out[1:]
    grad_sets = [deliver(grads[:4], section, 0), deliver(grads[4:], section, 4)]

    def assemble(sets, cut):
        near = jnp.concatenate([cut(b) for b in sets[0]], axis=1)
        far = jnp.concatenate([cut(b) for b in sets[1]], axis=1)
        return jnp.stack([jnp.where(first, near, far), jnp.where(first, far, near)])[:, None]

    acts_out = assemble(act_sets, lambda b: b)
    ingrad_out = assemble(grad_sets, lambda b: b[:, :COLS])
    keys = assemble(grad_sets, lambda b: b[:, COLS : COLS + HEAD_DIM])
    values = assemble(grad_sets, lambda b: b[:, COLS + HEAD_DIM :])
    return acts_out, ingrad_out, jnp.concatenate([keys, values], axis=-1)


def solution(mesh):
    in_specs = (
        P("seq", None),
        P("seq", None),
        P("seq", None),
        P("seq", None),
        P("section", None, None),
        P("section", None, None, None),
        P(),
    )
    out_specs = (
        P(None, "section", "seq", None),
        P(None, "section", "seq", None),
        P(None, "section", "seq", None),
    )
    return jax.shard_map(
        per_device, mesh=mesh, in_specs=in_specs, out_specs=out_specs, check_vma=False
    )
```
